32 devices in a mesh: groups: 2 (over y), width: 8 (over z, x), hidden: 2 (over core).
Axes of the slice: x: 2, y: 2, z: 4, core: 2. Of those that a mesh axis runs over, the one named last changes fastest.
Arguments:
- replay_store: bfloat16 [512, 8192], P('groups', 'width'), parts along dimension 0, may hold values from -18 to 18
- replay_ids: int32 [256], P('groups'), parts along dimension 0, may hold values from 0 to 255, as said below
- excluded: int32 [32], P('groups'), parts along dimension 0, may hold values from 0 to 127, as said below
- norm_gain: float32 [8192], P('width'), may hold values from 0.1 to 1.9
- w_gate: bfloat16 [8192, 14336], P('width', 'hidden'), may hold values from -0.0625 to 0.0625
- w_up: bfloat16 [8192, 14336], P('width', 'hidden'), may hold values from -0.0625 to 0.0625
- w_down: bfloat16 [14336, 8192], P('hidden', 'width'), may hold values from -0.046875 to 0.046875
- grad_out: bfloat16 [256, 8192], P('groups', 'width'), parts along dimension 0, may hold values from -6 to 6
Outputs:
- output: bfloat16 [256, 8192], P('groups', 'width'), parts along dimension 0
- store_grad: bfloat16 [512, 8192], P('groups', 'width'), parts along dimension 0
- gain_grad: float32 [16384], P(('groups', 'width')), parts along dimension 0
- gate_grad: bfloat16 [16384, 14336], P(('groups', 'width'), 'hidden'), parts along dimension 0
- up_grad: bfloat16 [16384, 14336], P(('groups', 'width'), 'hidden'), parts along dimension 0
- down_grad: bfloat16 [28672, 8192], P(('groups', 'hidden'), 'width'), parts along dimension 0
The draws below stay inside these ranges and needn't reach their ends.
There are 2 independent parts, one for each index of `groups`. The reference program is written for one: setup_inputs(seed, part) draws one part's arguments, and reference() takes and returns one part's arrays. A program takes and returns all parts, laid end to end along the dimension named above; an argument that names none is the same for every part. Nothing has to cross between parts.
Inputs may be any that keep to these rules, and one draw needn't show every extreme that they name: `replay_ids`: store rows may repeat; both ends of the range occur. `excluded`: positions may repeat; both ends of the range occur.
All inputs are finite; a program needn't handle non-finite values.
Results may differ from the reference program's by a relative error of at most 0.0068.
Values may be sent and summed in bfloat16 or wider, within the bound.
No kernel may reach another device: no remote copies, remote signals or barrier semaphores. Data moves between devices by JAX's collectives and lax.ppermute only.
A program may use at most 256 MiB of HBM per device.

```python
import math
import jax
import jax.numpy as jnp
from jax import lax

D = 8192
FF = 14336
TOK = 128
EXCL = 16
POOL = 256


def draw_replay_store(key, part):
    key = jax.random.fold_in(key, 11)
    k_base, k_row = jax.random.split(key, 2)
    column = jnp.arange(D, dtype=jnp.float32) / (D - 1)
    col_scale = jnp.exp(column * math.log(3.0))
    row_scale = jnp.exp(jax.random.uniform(k_row, (POOL, 1), jnp.float32) * math.log(10.0))
    base_draw = jnp.clip(jax.random.normal(k_base, (POOL, D), jnp.float32), -4.0, 4.0)
    return (0.15 * base_draw * col_scale * row_scale).astype(jnp.bfloat16)


def with_ends(key, count, upper):
    k_vals, k_first, k_step = jax.random.split(key, 3)
    values = jax.random.randint(k_vals, (count,), 0, upper, jnp.int32)
    first = jax.random.randint(k_first, (), 0, count, jnp.int32)
    second = (first + 1 + jax.random.randint(k_step, (), 0, count - 1, jnp.int32)) % count
    values = values.at[first].set(0)
    return values.at[second].set(upper - 1)


def draw_replay_ids(key, part):
    key = jax.random.fold_in(key, 21)
    return with_ends(key, TOK, POOL)


def draw_excluded(key, part):
    key = jax.random.fold_in(key, 31)
    return with_ends(key, EXCL, TOK)


def spiked(array, stream_key, source, target, parts, factor):
    def block_of(position):
        return (jnp.arange(array.shape[position]) // (array.shape[position] // parts)).reshape((-1,) + (1,) * (array.ndim - 1 - position))

    first = jax.random.permutation(stream_key, parts)[block_of(target)]
    far = (block_of(target) + parts // 2) % parts
    return jnp.where((block_of(source) == first) | (block_of(source) == far), factor * array, array)


def shard_levels(rng, shape, pieces, smallest, top_value):
    loudness, own = 1.0, jax.random.fold_in(rng, 6)
    for dim, parts in pieces:
        steps = jnp.exp(jax.random.uniform(jax.random.fold_in(own, dim), (parts,), jnp.float32, smallest / len(pieces), top_value / len(pieces)))
        loudness = loudness * jnp.repeat(steps, shape[dim] // parts).reshape([-1 if axis == dim else 1 for axis in range(len(shape))])
    return loudness


def noise(own_key, dims, deviation, reach, pieces=(), held_as=jnp.bfloat16):
    result = jax.random.normal(own_key, dims, jnp.float32) * deviation
    if len(pieces) > 0:
        result = shard_levels(own_key, dims, pieces, -0.22, 0.18) * result
    return jnp.clip(result, min=-reach, max=reach).astype(held_as)


def bell_draw_with(key, extent, deviation, limit, cuts, heavy, kind=jnp.bfloat16):
    drawn = deviation * jax.random.normal(key, extent, jnp.float32)
    if cuts:
        drawn = drawn * shard_levels(key, extent, cuts, -0.22, 0.18)
    return jnp.clip(spiked(drawn, jax.random.fold_in(key, 3), *heavy), -limit, limit).astype(kind)


def setup_inputs(seed: int = 0, part: int = 0) -> dict:
    splits = jax.random.split(jax.random.key(seed), 9)
    own_keys = jax.random.split(jax.random.fold_in(splits[8], part), 9)
    replay_store = draw_replay_store(jax.random.fold_in(jax.random.fold_in(splits[8], part), 71), part)
    replay_ids = draw_replay_ids(jax.random.fold_in(jax.random.fold_in(splits[8], part), 71), part)
    excluded = draw_excluded(jax.random.fold_in(jax.random.fold_in(splits[8], part), 71), part)
    norm_gain = jnp.clip(1.0 + 0.18 * jax.random.normal(splits[3], (D,), jnp.float32), 0.1, 1.9)
    w_gate = noise(splits[4], (D, FF), D ** -0.5, 0.0625, ((0, 8), (1, 2)))
    w_up = noise(splits[5], (D, FF), D ** -0.5, 0.0625, ((0, 8), (1, 2)))
    w_down = noise(splits[6], (FF, D), FF ** -0.5, 0.046875, ((0, 2), (1, 8)))
    grad_out = bell_draw_with(own_keys[7], (TOK, D), 1.0, 6.0, ((1, 8),), (1, 0, 8, 2.0))
    return {"replay_store": replay_store, "replay_ids": replay_ids, "excluded": excluded, "norm_gain": norm_gain, "w_gate": w_gate, "w_up": w_up, "w_down": w_down, "grad_out": grad_out}


EPS = 1e-05

def reference(replay_store, replay_ids, excluded, norm_gain, w_gate, w_up, w_down, grad_out):
    row_data = jnp.take(replay_store, replay_ids, axis=0)
    row_float = row_data.astype(jnp.float32)
    inv_rms = lax.rsqrt(lax.optimization_barrier(jnp.sum(row_float * row_float, axis=1, keepdims=True)) / D + EPS)
    normed = (row_float * inv_rms * norm_gain).astype(jnp.bfloat16)
    gate_pre = jnp.dot(normed, w_gate, preferred_element_type=jnp.float32)
    up_proj = jnp.dot(normed, w_up, preferred_element_type=jnp.float32)
    sigmoid_gate = jax.nn.sigmoid(gate_pre)
    silu_gate = gate_pre * sigmoid_gate
    hidden = (silu_gate * up_proj).astype(jnp.bfloat16)
    projected = jnp.dot(hidden, w_down, preferred_element_type=jnp.float32)
    output = (row_float + projected).astype(jnp.bfloat16)
    positions = jnp.arange(TOK, dtype=jnp.int32)
    dropped = jnp.any(positions[:, None] == excluded[None, :], axis=1)
    d_output = jnp.where(dropped[:, None], jnp.zeros_like(grad_out), grad_out)
    d_hidden = jnp.dot(d_output, w_down.T, preferred_element_type=jnp.float32)
    d_gate = (d_hidden * up_proj * sigmoid_gate * (1.0 + gate_pre * (1.0 - sigmoid_gate))).astype(jnp.bfloat16)
    d_up = (d_hidden * silu_gate).astype(jnp.bfloat16)
    down_grad = jnp.dot(hidden.T, d_output, preferred_element_type=jnp.float32).astype(jnp.bfloat16)
    gate_grad = jnp.dot(normed.T, d_gate, preferred_element_type=jnp.float32).astype(jnp.bfloat16)
    up_grad = jnp.dot(normed.T, d_up, preferred_element_type=jnp.float32).astype(jnp.bfloat16)
    d_normed = jnp.dot(d_gate, w_gate.T, preferred_element_type=jnp.float32) + jnp.dot(d_up, w_up.T, preferred_element_type=jnp.float32)
    gain_grad = lax.optimization_barrier(jnp.sum(d_normed * row_float * inv_rms, axis=0))
    scaled = d_normed * norm_gain
    inner_sum = lax.optimization_barrier(jnp.sum(scaled * row_float, axis=1, keepdims=True))
    d_rows = d_output.astype(jnp.float32) + inv_rms * scaled - row_float * inv_rms * inv_rms * inv_rms * (inner_sum / D)
    store_grad = jnp.zeros(replay_store.shape, jnp.float32).at[replay_ids].add(d_rows).astype(jnp.bfloat16)
    return (output, store_grad, gain_grad, gate_grad, up_grad, down_grad)
```

```python
import functools

import jax
import jax.numpy as jnp
from jax import lax
from jax.experimental import pallas as pl
from jax.experimental.pallas import tpu as pltpu
from jax.sharding import PartitionSpec as P

EPS = 1e-05
BF16 = jnp.bfloat16
F32 = jnp.float32
CHUNKS = 4
NT = (((1,), (1,)), ((), ()))
TN = (((0,), (0,)), ((), ()))
VMEM = pl.BlockSpec(memory_space=pltpu.VMEM)
SMEM = pl.BlockSpec(memory_space=pltpu.SMEM)
ANY = pl.BlockSpec(memory_space=pl.ANY)


def cost(flops, nbytes):
    return pl.CostEstimate(flops=int(flops), bytes_accessed=int(nbytes), transcendentals=0)


def params(mib):
    return pltpu.CompilerParams(vmem_limit_bytes=mib * 1024 * 1024)


def matmul(a, b, dims=(((1,), (0,)), ((), ()))):
    return lax.dot_general(a, b, dims, preferred_element_type=F32)


def tile_of(n):
    for t in (256, 128):
        if n % t == 0:
            return t
    return n


def order(label, tokens, block):
    p = lax.broadcasted_iota(jnp.int32, (tokens, tokens), 0)
    t = lax.broadcasted_iota(jnp.int32, (tokens, tokens), 1)
    return ((p // block) ^ label) * block + p % block == t


def start_kernel(block, label, store, ids, excluded, grad_out, rows, dout, squares):
    tokens = grad_out.shape[0]
    pool = store.shape[0]
    perm = jnp.where(order(label[0], tokens, block), 1.0, 0.0).astype(BF16)
    hit = lax.broadcasted_iota(jnp.int32, (pool, tokens), 0) == ids[...]
    natural = matmul(jnp.where(hit, 1.0, 0.0).astype(BF16), store[...], TN)
    total = jnp.sum(natural * natural, axis=1, keepdims=True)
    squares[...] = jnp.transpose(jnp.broadcast_to(total, (tokens, tokens)))[:1]
    rows[...] = matmul(perm, natural.astype(BF16)).astype(BF16)
    position = lax.broadcasted_iota(jnp.int32, (tokens, excluded.shape[1]), 0)
    match = jnp.where(position == excluded[...], 1.0, 0.0)
    dropped = jnp.max(match, axis=1, keepdims=True) > 0.0
    kept = jnp.where(dropped, 0.0, grad_out[...].astype(F32)).astype(BF16)
    dout[...] = matmul(perm, kept).astype(BF16)


def norm_kernel(block, width, label, rows, squares, gain, normed, flipped):
    tokens = rows.shape[0]
    inv = lax.rsqrt(squares[...] / width + EPS)
    inv = jnp.where(order(label[0], tokens, block), inv, 0.0)
    inv = jnp.sum(inv, axis=1, keepdims=True)
    value = (rows[...].astype(F32) * inv * gain[...]).astype(BF16)
    normed[...] = value
    flipped[...] = jnp.transpose(value.astype(F32)).astype(BF16)


def down_kernel(dout, w_down, keep, send):
    half = keep.shape[0]
    part = matmul(dout[...], w_down[...], NT)
    keep[...] = part[:half]
    send[...] = part[half:].astype(BF16)


def up_kernel(normed, w_gate, w_up, keep, send):
    half = keep.shape[1]
    for k, w in enumerate((w_gate, w_up)):
        part = matmul(normed[...], w[...])
        keep[k] = part[:half]
        send[k] = part[half:].astype(BF16)


def back_kernel(first, acts, flipped, dout, w_gate, w_up, w_down, *rest):
    acc, gate_grad, up_grad, down_grad = rest[-4:]

    @pl.when(pl.program_id(0) == 0)
    def _():
        acc[...] = jnp.zeros_like(acc) if first else rest[0][...]

    hidden, d_gate, d_up = acts[0], acts[1], acts[2]
    gate_grad[...] = matmul(flipped[...], d_gate).astype(BF16)
    up_grad[...] = matmul(flipped[...], d_up).astype(BF16)
    down_grad[...] = matmul(hidden, dout[...], TN).astype(BF16)
    acc[0] += matmul(hidden, w_down[...])
    acc[1] += matmul(d_gate, w_gate[...], NT) + matmul(d_up, w_up[...], NT)


def end_kernel(block, width, label, own, other, rows, dout, gain, squares, inner, ids, output, store_grad, gain_grad):
    tokens = rows.shape[0]
    pool = store_grad.shape[0]
    places = order(label[0], tokens, block)
    perm = jnp.where(places, 1.0, 0.0).astype(BF16)
    inv = lax.rsqrt(squares[...] / width + EPS)
    inv = jnp.sum(jnp.where(places, inv, 0.0), axis=1, keepdims=True)
    inner_sum = jnp.sum(jnp.where(places, inner[...], 0.0), axis=1, keepdims=True)
    row = rows[...].astype(F32)
    result = (row + (own[0] + other[0])).astype(BF16)
    output[...] = matmul(perm, result, TN).astype(BF16)
    d_normed = own[1] + other[1]
    gain_grad[...] = jnp.sum(d_normed * row * inv, axis=0, keepdims=True)
    d_rows = dout[...].astype(F32) + inv * (d_normed * gain[...]) - row * (inv * inv * (inner_sum / width))
    hit = lax.broadcasted_iota(jnp.int32, (pool, tokens), 0) == ids[...]
    target = matmul(jnp.where(hit, 1.0, 0.0).astype(BF16), perm, NT).astype(BF16)
    total = jnp.zeros(store_grad.shape, F32)
    for _ in range(3):
        piece = d_rows.astype(BF16)
        total += matmul(target, piece)
        d_rows = d_rows - piece.astype(F32)
    store_grad[...] = total.astype(BF16)


def shards(sizes, replay_store, replay_ids, excluded, norm_gain, w_gate, w_up, w_down, grad_out):
    ways = sizes["width"]
    steps = ways.bit_length() - 1
    tokens, d_here = grad_out.shape
    ff = w_down.shape[0]
    width = ways * d_here
    block = tokens // ways
    half = tokens // 2
    pool = replay_store.shape[0]
    part = ff // CHUNKS
    tile = tile_of(part)
    tiles = part // tile
    shape = jax.ShapeDtypeStruct

    index = lax.axis_index("width")
    label = sum(((index >> s) & 1) << (steps - 1 - s) for s in range(steps))
    label = jnp.reshape(label, (1,)).astype(jnp.int32)

    def swap(x, step):
        return lax.ppermute(x, "width", [(i, i ^ (1 << step)) for i in range(ways)])

    def swap_cores(x):
        n = sizes["hidden"]
        return lax.ppermute(x, "hidden", [(i, (i + 1) % n) for i in range(n)])

    def total_over_width(x):
        for step in range(steps):
            x = x + swap(x, step)
        return x

    ids = replay_ids.reshape(1, tokens)
    gain = norm_gain.reshape(1, d_here)
    rows, dout, squares = pl.pallas_call(
        functools.partial(start_kernel, block),
        out_shape=(shape((tokens, d_here), BF16), shape((tokens, d_here), BF16), shape((1, tokens), F32)),
        in_specs=[SMEM, VMEM, VMEM, VMEM, VMEM],
        out_specs=(VMEM, VMEM, VMEM),
        compiler_params=params(16),
        cost_estimate=cost(2 * tokens * pool * d_here, 2 * pool * d_here),
        name="start",
    )(label, replay_store, ids, excluded.reshape(1, -1), grad_out)

    d_tile = tile_of(ff)
    keep, send = pl.pallas_call(
        down_kernel,
        grid=(ff // d_tile,),
        out_shape=(shape((half, ff), F32), shape((half, ff), BF16)),
        in_specs=[
            pl.BlockSpec((tokens, d_here), lambda i: (0, 0)),
            pl.BlockSpec((d_tile, d_here), lambda i: (i, 0)),
        ],
        out_specs=(pl.BlockSpec((half, d_tile), lambda i: (0, i)), pl.BlockSpec((half, d_tile), lambda i: (0, i))),
        compiler_params=params(16),
        cost_estimate=cost(2 * tokens * ff * d_here, 2 * ff * d_here + 6 * half * ff),
        name="d_hidden",
    )(dout, w_down)

    squares = total_over_width(squares)
    normed, flipped = pl.pallas_call(
        functools.partial(norm_kernel, block, width),
        out_shape=(shape((tokens, d_here), BF16), shape((d_here, tokens), BF16)),
        in_specs=[SMEM, VMEM, VMEM, VMEM],
        out_specs=(VMEM, VMEM),
        compiler_params=params(16),
        cost_estimate=cost(tokens * d_here * 4, 6 * tokens * d_here),
        name="norm",
    )(label, rows, squares, gain)

    def reduce_tokens(keep, send):
        for step in range(steps):
            total = keep + swap(send, step).astype(F32)
            rest = total.shape[-2] // 2
            if step < steps - 1:
                keep, send = total[..., :rest, :], total[..., rest:, :].astype(BF16)
        return total

    def gather_tokens(x):
        for step in reversed(range(steps)):
            x = jnp.concatenate([x, swap(x, step)], axis=-2)
        return x

    d_hidden = reduce_tokens(keep, send)

    def pre(j):
        col = lambda i: (0, j * tiles + i)
        keep, send = pl.pallas_call(
            up_kernel,
            grid=(tiles,),
            out_shape=(shape((2, half, part), F32), shape((2, half, part), BF16)),
            in_specs=[
                pl.BlockSpec((tokens, d_here), lambda i: (0, 0)),
                pl.BlockSpec((d_here, tile), col),
                pl.BlockSpec((d_here, tile), col),
            ],
            out_specs=(
                pl.BlockSpec((2, half, tile), lambda i: (0, 0, i)),
                pl.BlockSpec((2, half, tile), lambda i: (0, 0, i)),
            ),
            compiler_params=params(16),
            cost_estimate=cost(4 * tokens * part * d_here, 4 * part * d_here + 12 * half * part),
            name="gate_up",
        )(normed, w_gate, w_up)
        return reduce_tokens(keep, send)

    inner = jnp.zeros((block,), F32)
    acts = []
    for j in range(CHUNKS):
        sums = pre(j)
        gate_pre, up_proj = sums[0], sums[1]
        d_part = d_hidden[:, j * part : (j + 1) * part]
        sigmoid_gate = jax.nn.sigmoid(gate_pre)
        silu = gate_pre * sigmoid_gate
        hidden = (silu * up_proj).astype(BF16)
        d_gate = (d_part * up_proj * sigmoid_gate * (1.0 + gate_pre * (1.0 - sigmoid_gate))).astype(BF16)
        d_up = (d_part * silu).astype(BF16)
        inner = inner + jnp.sum(d_gate.astype(F32) * gate_pre + d_up.astype(F32) * up_proj, axis=1)
        acts.append(gather_tokens(jnp.stack([hidden, d_gate, d_up])))

    inner = lax.dynamic_update_slice(jnp.zeros((1, tokens), F32), inner.reshape(1, block), (0, label[0] * block))
    inner = total_over_width(inner + swap_cores(inner))

    grads = None
    acc = None
    for j in range(CHUNKS):
        col = lambda i, j=j: (0, j * tiles + i)
        row = lambda i, j=j: (j * tiles + i, 0)
        whole = lambda i: (0, 0)
        acc_spec = pl.BlockSpec((2, tokens, d_here), lambda i: (0, 0, 0))
        first = j == 0
        extra = [] if first else [acc, *grads]
        acc, *grads = pl.pallas_call(
            functools.partial(back_kernel, first),
            grid=(tiles,),
            out_shape=(
                shape((2, tokens, d_here), F32),
                shape((d_here, ff), BF16),
                shape((d_here, ff), BF16),
                shape((ff, d_here), BF16),
            ),
            in_specs=[
                pl.BlockSpec((3, tokens, tile), lambda i: (0, 0, i)),
                pl.BlockSpec((d_here, tokens), whole),
                pl.BlockSpec((tokens, d_here), whole),
                pl.BlockSpec((d_here, tile), col),
                pl.BlockSpec((d_here, tile), col),
                pl.BlockSpec((tile, d_here), row),
            ]
            + ([] if first else [acc_spec, ANY, ANY, ANY]),
            out_specs=(
                acc_spec,
                pl.BlockSpec((d_here, tile), col),
                pl.BlockSpec((d_here, tile), col),
                pl.BlockSpec((tile, d_here), row),
            ),
            input_output_aliases={} if first else {7: 1, 8: 2, 9: 3},
            compiler_params=params(24),
            cost_estimate=cost(12 * tokens * part * d_here, 12 * part * d_here),
            name="back",
        )(acts[j], flipped, dout, w_gate, w_up, w_down, *extra)

    other = swap_cores(acc)
    output, store_grad, gain_grad = pl.pallas_call(
        functools.partial(end_kernel, block, width),
        out_shape=(shape((tokens, d_here), BF16), shape((pool, d_here), BF16), shape((1, d_here), F32)),
        in_specs=[SMEM] + [VMEM] * 8,
        out_specs=(VMEM, VMEM, VMEM),
        compiler_params=params(24),
        cost_estimate=cost(2 * tokens * pool * d_here, 16 * tokens * d_here),
        name="end",
    )(label, acc, other, rows, dout, gain, squares, inner, ids)
    return (output, store_grad, gain_grad.reshape(d_here), *grads)


def solution(mesh):
    return jax.shard_map(
        functools.partial(shards, dict(mesh.shape)),
        mesh=mesh,
        in_specs=(
            P("groups", "width"),
            P("groups"),
            P("groups"),
            P("width"),
            P("width", "hidden"),
            P("width", "hidden"),
            P("hidden", "width"),
            P("groups", "width"),
        ),
        out_specs=(
            P("groups", "width"),
            P("groups", "width"),
            P(("groups", "width")),
            P(("groups", "width"), "hidden"),
            P(("groups", "width"), "hidden"),
            P(("groups", "hidden"), "width"),
        ),
        check_vma=False,
    )
```

```python
import functools

import jax
import jax.numpy as jnp
from jax import lax
from jax.experimental import pallas as pl
from jax.experimental.pallas import tpu as pltpu
from jax.sharding import PartitionSpec as P

EPS = 1e-05
BF16 = jnp.bfloat16
F32 = jnp.float32
COUNTS = (2, 2, 2, 1)
SWAPPED = (False, False, False, False)
DOWN = ((0, 1), (2, 3))
ORDER = (
    ("D", 0), ("Q", 1), ("Q", 2), ("D", 1), ("N",), ("F", 0), ("F", 1), ("H", 0, 0), ("F", 2), ("H", 1, 0),
    ("H", 0, 1), ("F", 3), ("W", 0), ("H", 2, 0), ("H", 1, 1), ("J", 0, 2), ("W", 1), ("H", 2, 1),
    ("J", 0, 1), ("H", 3, 0), ("J", 1, 2), ("W", 2), ("H", 3, 1), ("J", 1, 1), ("J", 2, 2), ("B", 0),
    ("W", 3), ("J", 2, 1), ("J", 3, 2), ("B", 1), ("J", 3, 1), ("B", 2), ("B", 3),
)
START_MIB, HEAD_MIB, FORE_MIB, BACK_MIB = 60, 44, 44, 44
NT = (((1,), (1,)), ((), ()))
TN = (((0,), (0,)), ((), ()))
VMEM = pl.BlockSpec(memory_space=pltpu.VMEM)
SMEM = pl.BlockSpec(memory_space=pltpu.SMEM)
ANY = pl.BlockSpec(memory_space=pl.ANY)


def cost(flops, nbytes):
    return pl.CostEstimate(flops=int(flops), bytes_accessed=int(nbytes), transcendentals=0)


def params(mib):
    return pltpu.CompilerParams(vmem_limit_bytes=mib * 1024 * 1024)


def matmul(a, b, dims=(((1,), (0,)), ((), ()))):
    return lax.dot_general(a, b, dims, preferred_element_type=F32)


def order(label, tokens, block):
    p = lax.broadcasted_iota(jnp.int32, (tokens, tokens), 0)
    t = lax.broadcasted_iota(jnp.int32, (tokens, tokens), 1)
    return ((p // block) ^ label) * block + p % block == t


def split_rows(part, swapped):
    half = part.shape[0] // 2
    if not swapped:
        return part[:half], part[half:]
    q = half // 2
    return (
        jnp.concatenate([part[:q], part[half : half + q]], axis=0),
        jnp.concatenate([part[q:half], part[half + q :]], axis=0),
    )


def join_rows(own, other, swapped):
    if not swapped:
        return jnp.concatenate([own, other], axis=0)
    q = own.shape[0] // 2
    return jnp.concatenate([own[:q], other[:q], own[q:], other[q:]], axis=0)


def down_copies(spans, w_down, w_buf, sems):
    copies, at = [], 0
    for k, (first, size) in enumerate(spans):
        copies.append(pltpu.make_async_copy(w_down.at[pl.ds(first, size)], w_buf.at[pl.ds(at, size)], sems.at[k]))
        at += size
    return copies


def down_products(spans, copies, swapped, dout, w_buf, keep, send):
    at = 0
    for (_, size), copy in zip(spans, copies):
        copy.wait()
        here = slice(at, at + size)
        kept, sent = split_rows(matmul(dout[...], w_buf[here], NT), swapped)
        keep[0, :, here] = kept
        send[0, :, here] = sent.astype(BF16)
        at += size


def start_kernel(block, label, ids, excluded, store, grad_out, rows, dout, squares, pool_buf, grad_buf, sems):
    copies = [
        pltpu.make_async_copy(store, pool_buf, sems.at[0]),
        pltpu.make_async_copy(grad_out, grad_buf, sems.at[1]),
    ]
    for copy in copies:
        copy.start()
    tokens = grad_buf.shape[0]
    pool = pool_buf.shape[0]
    perm = jnp.where(order(label[0], tokens, block), 1.0, 0.0).astype(BF16)
    position = lax.broadcasted_iota(jnp.int32, (tokens, excluded.shape[1]), 0)
    match = jnp.where(position == excluded[...], 1.0, 0.0)
    dropped = jnp.max(match, axis=1, keepdims=True) > 0.0
    hit = lax.broadcasted_iota(jnp.int32, (pool, tokens), 0) == ids[...]
    hit = jnp.where(hit, 1.0, 0.0).astype(BF16)
    copies[0].wait()
    natural = matmul(hit, pool_buf[...], TN)
    total = jnp.sum(natural * natural, axis=1, keepdims=True)
    squares[...] = jnp.transpose(jnp.broadcast_to(total, (tokens, tokens)))[:1]
    rows[...] = matmul(perm, natural.astype(BF16)).astype(BF16)
    copies[1].wait()
    kept = jnp.where(dropped, 0.0, grad_buf[...].astype(F32)).astype(BF16)
    dout[...] = matmul(perm, kept).astype(BF16)


def down_kernel(spans, swapped, dout, w_down, *rest):
    keep, send, w_buf, sems = rest[-4:]
    copies = down_copies(spans, w_down, w_buf, sems)
    for copy in copies:
        copy.start()
    down_products(spans, copies, swapped, dout, w_buf, keep, send)


def add_kernel(own, other, *rest):
    rest[-1][...] = own[...] + other[...]


def norm_kernel(block, width, label, rows, squares, other, gain, *rest):
    normed, flipped, total = rest[-3:]
    tokens = rows.shape[0]
    total[...] = squares[...] + other[...]
    inv = lax.rsqrt(total[...] / width + EPS)
    inv = jnp.where(order(label[0], tokens, block), inv, 0.0)
    inv = jnp.sum(inv, axis=1, keepdims=True)
    value = (rows[...].astype(F32) * inv * gain[...]).astype(BF16)
    normed[...] = value
    flipped[...] = jnp.transpose(value.astype(F32)).astype(BF16)


def fore_kernel(swapped, normed, w_gate, w_up, *rest):
    keep, send = rest[-2:]
    for k, w in enumerate((w_gate, w_up)):
        kept, sent = split_rows(matmul(normed[...], w[...]), swapped)
        keep[k] = kept
        send[k] = sent.astype(BF16)


def halve_kernel(spans, *refs):
    keep, send = refs[-2:]
    rest = keep.shape[1]
    k = 0
    for n, span in enumerate(spans):
        kept, received = refs[2 * n], refs[2 * n + 1]
        for unit in range(kept.shape[0]):
            total = kept[unit, :, span] + received[unit, :, span].astype(F32)
            keep[k] = total[:rest]
            send[k] = total[rest:].astype(BF16)
            k += 1


def swiglu_kernel(last, kept, received, inner, *rest):
    acts, inner_out = rest[-2:]
    d_hidden, gate_pre, up_proj = (kept[k] + received[k].astype(F32) for k in range(3))
    part = gate_pre.shape[1]
    sigmoid_gate = jax.nn.sigmoid(gate_pre)
    silu = gate_pre * sigmoid_gate
    d_gate = (d_hidden * up_proj * sigmoid_gate * (1.0 + gate_pre * (1.0 - sigmoid_gate))).astype(BF16)
    d_up = (d_hidden * silu).astype(BF16)
    acts[0, :, :part] = (silu * up_proj).astype(BF16)
    acts[1, :, :part] = d_gate
    acts[2, :, :part] = d_up
    terms = d_gate.astype(F32) * gate_pre + d_up.astype(F32) * up_proj
    total = inner[...] + jnp.broadcast_to(jnp.sum(terms, axis=1, keepdims=True), inner.shape)
    inner_out[...] = total
    if last:
        for k in range(3):
            piece = total.astype(BF16)
            acts[k, :, part:] = piece
            total = total - piece.astype(F32)


def join_kernel(own, other, *rest):
    rows = own.shape[1]
    out = rest[-1]
    out[:, :rows] = own[...]
    out[:, rows:] = other[...]


def back_kernel(first, last, swapped, own, other, flipped, dout, w_gate, w_up, w_down, *rest):
    acc, gate_grad, up_grad, down_grad = rest[-4:]
    tokens = dout.shape[0]
    step = pl.program_id(0)

    @pl.when(step == 0)
    def _():
        acc[...] = jnp.zeros_like(acc) if first else rest[0][...]

    hidden, d_gate, d_up = (join_rows(own[k], other[k], swapped) for k in range(3))
    gate_grad[...] = matmul(flipped[...], d_gate).astype(BF16)
    up_grad[...] = matmul(flipped[...], d_up).astype(BF16)
    down_grad[...] = matmul(hidden, dout[...], TN).astype(BF16)
    acc[:tokens] += matmul(hidden, w_down[...])
    acc[tokens : 2 * tokens] += matmul(d_gate, w_gate[...], NT) + matmul(d_up, w_up[...], NT)
    if last:

        @pl.when(step == 0)
        def _():
            places = 0 if first else 4
            pieces = [sum(x[k].astype(F32) for k in range(3)) for x in rest[places : places + 2]]
            inner = jnp.transpose(join_rows(*pieces, swapped))[:8]
            acc[2 * tokens :, :tokens] = inner


def end_kernel(block, width, label, own, other, rows, dout, gain, squares, ids, output, store_grad, gain_grad):
    tokens = rows.shape[0]
    pool = store_grad.shape[0]
    places = order(label[0], tokens, block)
    perm = jnp.where(places, 1.0, 0.0).astype(BF16)
    inv = lax.rsqrt(squares[...] / width + EPS)
    inv = jnp.sum(jnp.where(places, inv, 0.0), axis=1, keepdims=True)
    here = lax.broadcasted_iota(jnp.int32, (tokens, tokens), 0) == lax.broadcasted_iota(jnp.int32, (tokens, tokens), 1)
    inner = own[2 * tokens : 2 * tokens + 1, :tokens] + other[2 * tokens : 2 * tokens + 1, :tokens]
    inner = jnp.sum(jnp.where(here, inner, 0.0), axis=1, keepdims=True)
    row = rows[...].astype(F32)
    result = (row + (own[:tokens] + other[:tokens])).astype(BF16)
    output[...] = matmul(perm, result, TN).astype(BF16)
    d_normed = own[tokens : 2 * tokens] + other[tokens : 2 * tokens]
    gain_grad[...] = jnp.sum(d_normed * row * inv, axis=0, keepdims=True)
    d_rows = dout[...].astype(F32) + inv * (d_normed * gain[...]) - row * (inv * inv * (inner / width))
    hit = lax.broadcasted_iota(jnp.int32, (pool, tokens), 0) == ids[...]
    target = matmul(jnp.where(hit, 1.0, 0.0).astype(BF16), perm, NT).astype(BF16)
    total = jnp.zeros(store_grad.shape, F32)
    for _ in range(3):
        piece = d_rows.astype(BF16)
        total += matmul(target, piece)
        d_rows = d_rows - piece.astype(F32)
    store_grad[...] = total.astype(BF16)


def shards(sizes, replay_store, replay_ids, excluded, norm_gain, w_gate, w_up, w_down, grad_out):
    ways = sizes["width"]
    steps = ways.bit_length() - 1
    tokens, d_here = grad_out.shape
    ff = w_down.shape[0]
    width = ways * d_here
    block = tokens // ways
    half = tokens // 2
    pool = replay_store.shape[0]
    tile = ff // sum(COUNTS)
    shape = jax.ShapeDtypeStruct

    index = lax.axis_index("width")
    label = sum(((index >> s) & 1) << (steps - 1 - s) for s in range(steps))
    label = jnp.reshape(label, (1,)).astype(jnp.int32)

    def swap(x, step):
        return lax.ppermute(x, "width", [(i, i ^ (1 << step)) for i in range(ways)])

    def swap_cores(x):
        n = sizes["hidden"]
        return lax.ppermute(x, "hidden", [(i, (i + 1) % n) for i in range(n)])

    ids = replay_ids.reshape(1, tokens)
    gain = norm_gain.reshape(1, d_here)
    routes = [[1, 0, *range(2, steps)] if swapped else list(range(steps)) for swapped in SWAPPED]
    chunks = len(COUNTS)
    parts = [count * tile for count in COUNTS]
    firsts = [sum(parts[:j]) for j in range(chunks)]
    token, held, arrived = [], [], {}

    def kernel(body, out_shape, in_specs, out_specs, ins, name, mib=24, flops=0, moved=0, **more):
        after = token[-1:] + held
        held.clear()
        outs = pl.pallas_call(
            body,
            out_shape=out_shape,
            in_specs=list(in_specs) + [ANY] * len(after),
            out_specs=out_specs,
            compiler_params=params(mib),
            cost_estimate=cost(0, 0),
            name=name,
            **more,
        )(*ins, *after)
        token.append(outs[0])
        return outs

    def down_shapes(group):
        wide = sum(parts[j] for j in group)
        return (shape((1, half, wide), F32), shape((1, half, wide), BF16)), [
            pltpu.VMEM((wide, d_here), BF16),
            pltpu.SemaphoreType.DMA((len(group),)),
        ]

    down_parts = {}

    def down_done(g, group, keep, send):
        recv = arrived["D", g] = swap(send, routes[group[0]][0])
        at = 0
        for j in group:
            down_parts[j] = (keep, recv, slice(at, at + parts[j]))
            at += parts[j]

    rows, dout, squares = kernel(
        functools.partial(start_kernel, block),
        (shape((tokens, d_here), BF16), shape((tokens, d_here), BF16), shape((1, tokens), F32)),
        [SMEM, VMEM, VMEM, ANY, ANY],
        (VMEM,) * 3,
        [label, ids, excluded.reshape(1, -1), replay_store, grad_out],
        "start",
        mib=START_MIB,
        scratch_shapes=[
            pltpu.VMEM((pool, d_here), BF16),
            pltpu.VMEM((tokens, d_here), BF16),
            pltpu.SemaphoreType.DMA((2,)),
        ],
    )

    def down(g):
        group = DOWN[g]
        out_shape, scratch = down_shapes(group)
        spans = [(firsts[j], parts[j]) for j in group]
        keep, send = kernel(
            functools.partial(down_kernel, spans, SWAPPED[group[0]]),
            out_shape,
            [VMEM, ANY],
            (VMEM, VMEM),
            [dout, w_down],
            "d_hidden",
            mib=HEAD_MIB,
            scratch_shapes=scratch,
        )
        down_done(g, group, keep, send)

    state = {"inner": jnp.zeros((block, 128), F32), "acc": None, "grads": None, "swiglu": 0, "back": 0}
    state["squares"] = squares

    arrived["Q", 0] = swap(squares, 0)

    def square(step):
        for k in range(step, steps if step == 2 else step + 1):
            (state["squares"],) = kernel(
                add_kernel,
                (shape((1, tokens), F32),),
                [VMEM, VMEM],
                (VMEM,),
                [state["squares"], arrived["Q", min(k, 3) - 1]],
                "squares",
            )
            arrived["Q", min(k, 2)] = swap(state["squares"], k)

    def norm():
        normed, flipped, state["squares"] = kernel(
            functools.partial(norm_kernel, block, width),
            (shape((tokens, d_here), BF16), shape((d_here, tokens), BF16), shape((1, tokens), F32)),
            [SMEM, VMEM, VMEM, VMEM, VMEM],
            (VMEM, VMEM, VMEM),
            [label, rows, state["squares"], arrived["Q", 2], gain],
            "norm",
        )
        return normed, flipped

    sums, acts, others = {}, {}, {}
    def fore(j):
        part = parts[j]
        out = pl.BlockSpec((2, half, tile), lambda i: (0, 0, i))
        col = pl.BlockSpec((d_here, tile), lambda i: (0, firsts[j] // tile + i))
        keep, send = kernel(
            functools.partial(fore_kernel, SWAPPED[j]),
            (shape((2, half, part), F32), shape((2, half, part), BF16)),
            [pl.BlockSpec((tokens, d_here), lambda i: (0, 0)), col, col],
            (out, out),
            [state["normed"][0], w_gate, w_up],
            "gate_up",
            mib=FORE_MIB,
            flops=4 * tokens * part * d_here,
            moved=4 * part * d_here,
            grid=(COUNTS[j],),
        )
        arrived["F", j] = swap(send, routes[j][0])
        sums[j] = [down_parts[j], (keep, arrived["F", j], slice(0, part))]

    def halve(j, at):
        for step in range(at, steps - 1 if at else 1):
            pairs = sums[j]
            units = sum(kept.shape[0] for kept, _, _ in pairs)
            rows_here = pairs[0][0].shape[1]
            part = parts[j]
            keep, send = kernel(
                functools.partial(halve_kernel, [span for _, _, span in pairs]),
                (shape((units, rows_here // 2, part), F32), shape((units, rows_here // 2, part), BF16)),
                [VMEM] * (2 * len(pairs)),
                (VMEM, VMEM),
                [x for kept, received, _ in pairs for x in (kept, received)],
                "halve",
            )
            arrived["H", j, at] = swap(send, routes[j][step + 1])
            sums[j] = [(keep, arrived["H", j, at], slice(0, part))]

    def swiglu(j):
        state["swiglu"] += 1
        last = state["swiglu"] == chunks
        state["last"] = j if last else None
        keep, recv, _ = sums[j][0]
        acts[j], state["inner"] = kernel(
            functools.partial(swiglu_kernel, last),
            (shape((3, block, parts[j] + (128 if last else 0)), BF16), shape((block, 128), F32)),
            [VMEM] * 3,
            (VMEM, VMEM),
            [keep, recv, state["inner"]],
            "swiglu",
        )
        others[j] = arrived["W", j] = swap(acts[j], routes[j][steps - 1])

    def join(j, at):
        for step in reversed(range(at, steps if at > 1 else 2)):
            own, other = acts[j], others[j]
            if own.shape[1] % 16:
                acts[j] = jnp.concatenate([own, other], axis=1)
            else:
                (acts[j],) = kernel(
                    join_kernel,
                    (shape((3, 2 * own.shape[1], own.shape[2]), BF16),),
                    [VMEM, VMEM],
                    (VMEM,),
                    [own, other],
                    "join",
                )
            others[j] = arrived["J", j, at] = swap(acts[j], routes[j][step - 1])

    def back(j):
        state["back"] += 1
        first, last = state["back"] == 1, j == state["last"]
        own, other = acts[j], others[j]
        start = firsts[j] // tile
        col = pl.BlockSpec((d_here, tile), lambda i: (0, start + i))
        row = pl.BlockSpec((tile, d_here), lambda i: (start + i, 0))
        whole = lambda i: (0, 0)
        acc_spec = pl.BlockSpec((2 * tokens + 8, d_here), whole)
        piece = pl.BlockSpec((3, half, tile), lambda i: (0, 0, i))
        ins = [own, other, state["normed"][1], dout, w_gate, w_up, w_down]
        specs = [
            piece,
            piece,
            pl.BlockSpec((d_here, tokens), whole),
            pl.BlockSpec((tokens, d_here), whole),
            col,
            col,
            row,
        ]
        alias = {}
        if not first:
            ins += [state["acc"], *state["grads"]]
            specs += [acc_spec, ANY, ANY, ANY]
            alias = {8: 1, 9: 2, 10: 3}
        if last:
            extra = pl.BlockSpec((3, half, 128), lambda i: (0, 0, parts[j] // 128))
            ins += [own, other]
            specs += [extra, extra]
        state["acc"], *state["grads"] = kernel(
            functools.partial(back_kernel, first, last, SWAPPED[j]),
            (
                shape((2 * tokens + 8, d_here), F32),
                shape((d_here, ff), BF16),
                shape((d_here, ff), BF16),
                shape((ff, d_here), BF16),
            ),
            specs,
            (acc_spec, col, col, row),
            ins,
            "back",
            mib=BACK_MIB,
            flops=12 * tokens * parts[j] * d_here,
            moved=12 * parts[j] * d_here,
            grid=(COUNTS[j],),
            input_output_aliases=alias,
        )

    tasks = {"D": down, "Q": square, "F": fore, "H": halve, "W": swiglu, "J": join, "B": back}
    for task, *where in ORDER:
        if task == "A":
            held.append(arrived[tuple(where)])
        elif task == "N":
            state["normed"] = norm()
        else:
            tasks[task](*where)
    acc, grads = state["acc"], state["grads"]

    other = swap_cores(acc)
    output, store_grad, gain_grad = pl.pallas_call(
        functools.partial(end_kernel, block, width),
        out_shape=(shape((tokens, d_here), BF16), shape((pool, d_here), BF16), shape((1, d_here), F32)),
        in_specs=[SMEM] + [VMEM] * 7,
        out_specs=(VMEM, VMEM, VMEM),
        compiler_params=params(32),
        cost_estimate=cost(2 * tokens * pool * d_here, 16 * tokens * d_here),
        name="end",
    )(label, acc, other, rows, dout, gain, state["squares"], ids)
    return (output, store_grad, gain_grad.reshape(d_here), *grads)


def solution(mesh):
    return jax.shard_map(
        functools.partial(shards, dict(mesh.shape)),
        mesh=mesh,
        in_specs=(
            P("groups", "width"),
            P("groups"),
            P("groups"),
            P("width"),
            P("width", "hidden"),
            P("width", "hidden"),
            P("hidden", "width"),
            P("groups", "width"),
        ),
        out_specs=(
            P("groups", "width"),
            P("groups", "width"),
            P(("groups", "width")),
            P(("groups", "width"), "hidden"),
            P(("groups", "width"), "hidden"),
            P(("groups", "hidden"), "width"),
        ),
        check_vma=False,
    )
```

```python
import functools

import jax
import jax.numpy as jnp
from jax import lax
from jax.experimental import pallas as pl
from jax.experimental.pallas import tpu as pltpu
from jax.sharding import PartitionSpec as P

EPS = 1e-05
BF16 = jnp.bfloat16
F32 = jnp.float32
COUNTS = (2, 2, 2, 1)
SWAPPED = (False, False, False, False)
ORDER = (
    ("F", 1),
    ("H", 0, 0),
    ("F", 2),
    ("H", 0, 1),
    ("H", 1, 0),
    ("F", 3),
    ("W", 0),
    ("J", 0, 2),
    ("H", 1, 1),
    ("H", 2, 0),
    ("J", 0, 1),
    ("W", 1),
    ("J", 1, 2),
    ("H", 2, 1),
    ("H", 3, 0),
    ("W", 2),
    ("H", 3, 1),
    ("J", 1, 1),
    ("J", 2, 2),
    ("B", 0),
    ("W", 3),
    ("J", 2, 1),
    ("J", 3, 2),
    ("B", 1),
    ("J", 3, 1),
    ("B", 2),
    ("B", 3),
)
COSTS = (0,) * len(ORDER)
START_MIB, FORE_MIB, BACK_MIB = 44, 44, 44
NN = (((1,), (0,)), ((), ()))
NT = (((1,), (1,)), ((), ()))
TN = (((0,), (0,)), ((), ()))
VMEM = pl.BlockSpec(memory_space=pltpu.VMEM)
SMEM = pl.BlockSpec(memory_space=pltpu.SMEM)
ANY = pl.BlockSpec(memory_space=pl.ANY)


def cost(flops, nbytes):
    return pl.CostEstimate(flops=int(flops), bytes_accessed=int(nbytes), transcendentals=0)


def params(mib):
    return pltpu.CompilerParams(vmem_limit_bytes=mib * 1024 * 1024)


def matmul(a, b, dims=NN):
    return lax.dot_general(a, b, dims, preferred_element_type=F32)


def order(label, tokens, block):
    p = lax.broadcasted_iota(jnp.int32, (tokens, tokens), 0)
    t = lax.broadcasted_iota(jnp.int32, (tokens, tokens), 1)
    return ((p // block) ^ label) * block + p % block == t


def split_rows(part, swapped):
    half = part.shape[0] // 2
    if not swapped:
        return part[:half], part[half:]
    q = half // 2
    return (
        jnp.concatenate([part[:q], part[half : half + q]], axis=0),
        jnp.concatenate([part[q:half], part[half + q :]], axis=0),
    )


def join_rows(own, other, swapped):
    if not swapped:
        return jnp.concatenate([own, other], axis=0)
    q = own.shape[0] // 2
    return jnp.concatenate([own[:q], other[:q], own[q:], other[q:]], axis=0)


def start_kernel(block, span, tile, swapped, label, ids, excluded, gain, store, grad_out, w_down, w_gate, w_up, *rest):
    rows, dout, scaled, flipped, keep, send, pool_buf, grad_buf, wd, wg, wu, sems, w_sems = rest
    copies = [
        pltpu.make_async_copy(store, pool_buf, sems.at[0]),
        pltpu.make_async_copy(grad_out, grad_buf, sems.at[1]),
    ]
    w_copies = []
    for at in range(0, span[1], tile):
        there, here = pl.ds(span[0] + at, tile), pl.ds(at, tile)
        n = len(w_copies)
        w_copies.append(pltpu.make_async_copy(w_down.at[there], wd.at[here], w_sems.at[n]))
        w_copies.append(pltpu.make_async_copy(w_gate.at[:, there], wg.at[:, here], w_sems.at[n + 1]))
        w_copies.append(pltpu.make_async_copy(w_up.at[:, there], wu.at[:, here], w_sems.at[n + 2]))
    for copy in copies + w_copies:
        copy.start()
    tokens = grad_buf.shape[0]
    pool = pool_buf.shape[0]
    perm = jnp.where(order(label[0], tokens, block), 1.0, 0.0).astype(BF16)
    position = lax.broadcasted_iota(jnp.int32, (tokens, excluded.shape[1]), 0)
    match = jnp.where(position == excluded[...], 1.0, 0.0)
    dropped = jnp.max(match, axis=1, keepdims=True) > 0.0
    hit = lax.broadcasted_iota(jnp.int32, (pool, tokens), 0) == ids[...]
    hit = jnp.where(hit, 1.0, 0.0).astype(BF16)
    copies[0].wait()
    natural = matmul(hit, pool_buf[...], TN)
    row = matmul(perm, natural.astype(BF16))
    squares = jnp.broadcast_to(jnp.sum(row * row, axis=1, keepdims=True), (tokens, 128))
    put_pieces(*split_rows(squares, swapped), keep, send, span[1])
    rows[...] = row.astype(BF16)
    value = (row * gain[...]).astype(BF16)
    scaled[...] = value
    flipped[...] = jnp.transpose(value.astype(F32)).astype(BF16)
    copies[1].wait()
    kept = jnp.where(dropped, 0.0, grad_buf[...].astype(F32)).astype(BF16)
    dout[...] = matmul(perm, kept).astype(BF16)
    for n, copy in enumerate(w_copies):
        copy.wait()
        k = n % 3
        here = slice(n // 3 * tile, (n // 3 + 1) * tile)
        part = matmul(dout[...], wd[here], NT) if k == 0 else matmul(scaled[...], (wg if k == 1 else wu)[:, here])
        kept, sent = split_rows(part, swapped)
        keep[k, :, here] = kept
        send[k, :, here] = sent.astype(BF16)


def put_pieces(kept, sent, keep, send, at):
    for k in range(3):
        keep[k, :, at:] = kept if k == 0 else jnp.zeros_like(kept)
        piece = sent.astype(BF16)
        send[k, :, at:] = piece
        sent = sent - piece.astype(F32)


def fore_kernel(swapped, refs, keep, send):
    for k, (x, w, dims) in enumerate(refs):
        kept, sent = split_rows(matmul(x[...], w[...], dims), swapped)
        keep[k] = kept
        send[k] = sent.astype(BF16)


def all_kernel(swapped, normed, dout, w_down, w_gate, w_up, *rest):
    fore_kernel(swapped, [(dout, w_down, NT), (normed, w_gate, NN), (normed, w_up, NN)], *rest[-2:])


def halve_kernel(part, kept, received, *rest):
    keep, send = rest[-2:]
    rows = keep.shape[1]
    for k in range(3):
        total = kept[k, :, :part] + received[k, :, :part].astype(F32)
        keep[k, :, :part] = total[:rows]
        send[k, :, :part] = total[rows:].astype(BF16)
    if keep.shape[2] > part:
        total = sum(kept[k, :, part:] + received[k, :, part:].astype(F32) for k in range(3))
        put_pieces(total[:rows], total[rows:], keep, send, part)


def swiglu_kernel(part, last, width, kept, received, inner, inv_rms, *rest):
    acts, inner_out, inv_out = rest[-3:]
    d_hidden, gate_pre, up_proj = (kept[k, :, :part] + received[k, :, :part].astype(F32) for k in range(3))
    if kept.shape[2] > part:
        squares = sum(kept[k, :, part:] + received[k, :, part:].astype(F32) for k in range(3))
        inv = lax.rsqrt(squares / width + EPS)
    else:
        inv = inv_rms[...]
    inv_out[...] = inv
    inv = inv[:, :1]
    gate_pre = gate_pre * inv
    up_proj = up_proj * inv
    sigmoid_gate = jax.nn.sigmoid(gate_pre)
    silu = gate_pre * sigmoid_gate
    d_scaled = d_hidden * inv
    d_gate = (d_scaled * up_proj * sigmoid_gate * (1.0 + gate_pre * (1.0 - sigmoid_gate))).astype(BF16)
    d_up = (d_scaled * silu).astype(BF16)
    acts[0, :, :part] = (silu * up_proj).astype(BF16)
    acts[1, :, :part] = d_gate
    acts[2, :, :part] = d_up
    terms = d_gate.astype(F32) * gate_pre + d_up.astype(F32) * up_proj
    total = inner[...] + jnp.broadcast_to(inv * jnp.sum(terms, axis=1, keepdims=True), inner.shape)
    inner_out[...] = total
    if last:
        for k in range(3):
            piece = total.astype(BF16)
            acts[k, :, part:] = piece
            total = total - piece.astype(F32)


def join_kernel(own, other, *rest):
    rows = own.shape[1]
    out = rest[-1]
    out[:, :rows] = own[...]
    out[:, rows:] = other[...]


def back_kernel(first, last, swapped, own, other, flipped, dout, w_gate, w_up, w_down, *rest):
    acc, gate_grad, up_grad, down_grad = rest[-4:]
    tokens = dout.shape[0]
    step = pl.program_id(0)

    @pl.when(step == 0)
    def _():
        acc[...] = jnp.zeros_like(acc) if first else rest[0][...]

    hidden, d_gate, d_up = (join_rows(own[k], other[k], swapped) for k in range(3))
    gate_grad[...] = matmul(flipped[...], d_gate).astype(BF16)
    up_grad[...] = matmul(flipped[...], d_up).astype(BF16)
    down_grad[...] = matmul(hidden, dout[...], TN).astype(BF16)
    acc[:tokens] += matmul(hidden, w_down[...])
    acc[tokens : 2 * tokens] += matmul(d_gate, w_gate[...], NT) + matmul(d_up, w_up[...], NT)
    if last:

        @pl.when(step == 0)
        def _():
            places = 0 if first else 4
            pieces = [sum(x[k].astype(F32) for k in range(3)) for x in rest[places : places + 2]]
            inner = jnp.transpose(join_rows(*pieces, swapped))[:8]
            acc[2 * tokens :, :tokens] = inner


def end_kernel(block, width, label, own, other, rows, dout, gain, ids, output, store_grad, gain_grad):
    tokens = rows.shape[0]
    pool = store_grad.shape[0]
    places = order(label[0], tokens, block)
    perm = jnp.where(places, 1.0, 0.0).astype(BF16)
    here = lax.broadcasted_iota(jnp.int32, (tokens, tokens), 0) == lax.broadcasted_iota(jnp.int32, (tokens, tokens), 1)
    inner = own[2 * tokens : 2 * tokens + 1, :tokens] + other[2 * tokens : 2 * tokens + 1, :tokens]
    inner = jnp.sum(jnp.where(here, inner, 0.0), axis=1, keepdims=True)
    row = rows[...].astype(F32)
    result = (row + (own[:tokens] + other[:tokens])).astype(BF16)
    output[...] = matmul(perm, result, TN).astype(BF16)
    d_normed = own[tokens : 2 * tokens] + other[tokens : 2 * tokens]
    gain_grad[...] = jnp.sum(d_normed * row, axis=0, keepdims=True)
    d_rows = dout[...].astype(F32) + d_normed * gain[...] - row * (inner / width)
    hit = lax.broadcasted_iota(jnp.int32, (pool, tokens), 0) == ids[...]
    target = matmul(jnp.where(hit, 1.0, 0.0).astype(BF16), perm, NT).astype(BF16)
    total = jnp.zeros(store_grad.shape, F32)
    for _ in range(3):
        piece = d_rows.astype(BF16)
        total += matmul(target, piece)
        d_rows = d_rows - piece.astype(F32)
    store_grad[...] = total.astype(BF16)


def shards(sizes, replay_store, replay_ids, excluded, norm_gain, w_gate, w_up, w_down, grad_out):
    ways = sizes["width"]
    steps = ways.bit_length() - 1
    tokens, d_here = grad_out.shape
    ff = w_down.shape[0]
    width = ways * d_here
    block = tokens // ways
    half = tokens // 2
    pool = replay_store.shape[0]
    tile = ff // sum(COUNTS)
    shape = jax.ShapeDtypeStruct

    index = lax.axis_index("width")
    label = sum(((index >> s) & 1) << (steps - 1 - s) for s in range(steps))
    label = jnp.reshape(label, (1,)).astype(jnp.int32)

    def swap(x, step):
        return lax.ppermute(x, "width", [(i, i ^ (1 << step)) for i in range(ways)])

    def swap_cores(x):
        n = sizes["hidden"]
        return lax.ppermute(x, "hidden", [(i, (i + 1) % n) for i in range(n)])

    ids = replay_ids.reshape(1, tokens)
    gain = norm_gain.reshape(1, d_here)
    routes = [[1, 0, *range(2, steps)] if swapped else list(range(steps)) for swapped in SWAPPED]
    chunks = len(COUNTS)
    parts = [count * tile for count in COUNTS]
    firsts = [sum(parts[:j]) for j in range(chunks)]
    token, held, arrived = [], [], {}

    state = {"cost": 0}

    def kernel(body, out_shape, in_specs, out_specs, ins, name, mib=24, **more):
        after = token[-1:] + held
        held.clear()
        outs = pl.pallas_call(
            body,
            out_shape=out_shape,
            in_specs=list(in_specs) + [ANY] * len(after),
            out_specs=out_specs,
            compiler_params=params(mib),
            cost_estimate=cost(0, 1e6 * state["cost"]),
            name=name,
            **more,
        )(*ins, *after)
        token.append(outs[0])
        return outs

    part = parts[0]
    side = pltpu.VMEM((d_here, part), BF16)
    rows, dout, scaled, flipped, keep, send = kernel(
        functools.partial(start_kernel, block, (firsts[0], part), tile, SWAPPED[0]),
        (
            shape((tokens, d_here), BF16),
            shape((tokens, d_here), BF16),
            shape((tokens, d_here), BF16),
            shape((d_here, tokens), BF16),
            shape((3, half, part + 128), F32),
            shape((3, half, part + 128), BF16),
        ),
        [SMEM, VMEM, VMEM, VMEM] + [ANY] * 5,
        (VMEM,) * 6,
        [label, ids, excluded.reshape(1, -1), gain, replay_store, grad_out, w_down, w_gate, w_up],
        "start",
        mib=START_MIB,
        scratch_shapes=[
            pltpu.VMEM((pool, d_here), BF16),
            pltpu.VMEM((tokens, d_here), BF16),
            pltpu.VMEM((part, d_here), BF16),
            side,
            side,
            pltpu.SemaphoreType.DMA((2,)),
            pltpu.SemaphoreType.DMA((3 * COUNTS[0],)),
        ],
    )
    zeros = jnp.zeros((block, 128), F32)
    state |= {"inner": zeros, "inv": zeros, "acc": None, "grads": None, "swiglu": 0, "back": 0}
    arrived["F", 0] = swap(send, routes[0][0])
    sums, acts, others = {0: (keep, arrived["F", 0])}, {}, {}

    def fore(j):
        part = parts[j]
        whole = pl.BlockSpec((tokens, d_here), lambda i: (0, 0))
        col = pl.BlockSpec((d_here, tile), lambda i: (0, firsts[j] // tile + i))
        row = pl.BlockSpec((tile, d_here), lambda i: (firsts[j] // tile + i, 0))
        n = 3
        out = pl.BlockSpec((n, half, tile), lambda i: (0, 0, i))
        keep, send = kernel(
            functools.partial(all_kernel, SWAPPED[j]),
            (shape((n, half, part), F32), shape((n, half, part), BF16)),
            [whole, whole, row, col, col],
            (out, out),
            [scaled, dout, w_down, w_gate, w_up],
            "fore",
            mib=FORE_MIB,
            grid=(COUNTS[j],),
        )
        arrived["F", j] = swap(send, routes[j][0])
        sums[j] = keep, arrived["F", j]

    def halve(j, at):
        for step in range(at, steps - 1 if at else 1):
            kept, received = sums[j]
            here = (3, kept.shape[1] // 2, kept.shape[2])
            keep, send = kernel(
                functools.partial(halve_kernel, parts[j]),
                (shape(here, F32), shape(here, BF16)),
                [VMEM, VMEM],
                (VMEM, VMEM),
                [kept, received],
                "halve",
            )
            arrived["H", j, at] = swap(send, routes[j][step + 1])
            sums[j] = keep, arrived["H", j, at]

    def swiglu(j):
        state["swiglu"] += 1
        last = state["swiglu"] == chunks
        state["last"] = j if last else None
        acts[j], state["inner"], state["inv"] = kernel(
            functools.partial(swiglu_kernel, parts[j], last, width),
            (shape((3, block, parts[j] + (128 if last else 0)), BF16), shape((block, 128), F32), shape((block, 128), F32)),
            [VMEM] * 4,
            (VMEM,) * 3,
            [*sums[j], state["inner"], state["inv"]],
            "swiglu",
        )
        others[j] = arrived["W", j] = swap(acts[j], routes[j][steps - 1])

    def join(j, at):
        for step in reversed(range(at, steps if at > 1 else 2)):
            own, other = acts[j], others[j]
            if own.shape[1] % 16:
                acts[j] = jnp.concatenate([own, other], axis=1)
            else:
                (acts[j],) = kernel(
                    join_kernel,
                    (shape((3, 2 * own.shape[1], own.shape[2]), BF16),),
                    [VMEM, VMEM],
                    (VMEM,),
                    [own, other],
                    "join",
                )
            others[j] = arrived["J", j, at] = swap(acts[j], routes[j][step - 1])

    def back(j):
        state["back"] += 1
        first, last = state["back"] == 1, j == state["last"]
        own, other = acts[j], others[j]
        start = firsts[j] // tile
        col = pl.BlockSpec((d_here, tile), lambda i: (0, start + i))
        row = pl.BlockSpec((tile, d_here), lambda i: (start + i, 0))
        whole = lambda i: (0, 0)
        acc_spec = pl.BlockSpec((2 * tokens + 8, d_here), whole)
        piece = pl.BlockSpec((3, half, tile), lambda i: (0, 0, i))
        ins = [own, other, flipped, dout, w_gate, w_up, w_down]
        specs = [
            piece,
            piece,
            pl.BlockSpec((d_here, tokens), whole),
            pl.BlockSpec((tokens, d_here), whole),
            col,
            col,
            row,
        ]
        alias = {}
        if not first:
            ins += [state["acc"], *state["grads"]]
            specs += [acc_spec, ANY, ANY, ANY]
            alias = {8: 1, 9: 2, 10: 3}
        if last:
            extra = pl.BlockSpec((3, half, 128), lambda i: (0, 0, parts[j] // 128))
            ins += [own, other]
            specs += [extra, extra]
        state["acc"], *state["grads"] = kernel(
            functools.partial(back_kernel, first, last, SWAPPED[j]),
            (
                shape((2 * tokens + 8, d_here), F32),
                shape((d_here, ff), BF16),
                shape((d_here, ff), BF16),
                shape((ff, d_here), BF16),
            ),
            specs,
            (acc_spec, col, col, row),
            ins,
            "back",
            mib=BACK_MIB,
            grid=(COUNTS[j],),
            input_output_aliases=alias,
        )

    tasks = {"F": fore, "H": halve, "W": swiglu, "J": join, "B": back}
    for (task, *where), state["cost"] in zip(ORDER, COSTS):
        if task == "A":
            held.append(arrived[tuple(where)])
        else:
            tasks[task](*where)
    acc, grads = state["acc"], state["grads"]

    other = swap_cores(acc)
    output, store_grad, gain_grad = pl.pallas_call(
        functools.partial(end_kernel, block, width),
        out_shape=(shape((tokens, d_here), BF16), shape((pool, d_here), BF16), shape((1, d_here), F32)),
        in_specs=[SMEM] + [VMEM] * 6,
        out_specs=(VMEM, VMEM, VMEM),
        compiler_params=params(32),
        cost_estimate=cost(2 * tokens * pool * d_here, 16 * tokens * d_here),
        name="end",
    )(label, acc, other, rows, dout, gain, ids)
    return (output, store_grad, gain_grad.reshape(d_here), *grads)


def solution(mesh):
    return jax.shard_map(
        functools.partial(shards, dict(mesh.shape)),
        mesh=mesh,
        in_specs=(
            P("groups", "width"),
            P("groups"),
            P("groups"),
            P("width"),
            P("width", "hidden"),
            P("width", "hidden"),
            P("hidden", "width"),
            P("groups", "width"),
        ),
        out_specs=(
            P("groups", "width"),
            P("groups", "width"),
            P(("groups", "width")),
            P(("groups", "width"), "hidden"),
            P(("groups", "width"), "hidden"),
            P(("groups", "hidden"), "width"),
        ),
        check_vma=False,
    )
```

```python
import functools

import jax
import jax.numpy as jnp
from jax import lax
from jax.experimental import pallas as pl
from jax.experimental.pallas import tpu as pltpu
from jax.sharding import PartitionSpec as P

EPS = 1e-05
BF16 = jnp.bfloat16
F32 = jnp.float32
COUNTS = (2, 2, 2, 1)
SWAPPED = (False, False, False, False)
ORDER = (
    ("F", 2), ("F", 1), ("H", 0, 0), ("H", 0, 1), ("H", 1, 0), ("F", 3), ("W", 0), ("H", 2, 0), ("J", 0, 2),
    ("H", 1, 1), ("H", 2, 1), ("H", 3, 0), ("W", 1), ("J", 0, 1), ("J", 1, 2), ("H", 3, 1), ("W", 2),
    ("A", "W", 2), ("J", 1, 1), ("J", 2, 2), ("B", 0), ("W", 3), ("J", 2, 1), ("J", 3, 2), ("B", 1),
    ("J", 3, 1), ("B", 2), ("B", 3),
)
COSTS = (
    0, 20, 0, 0, 8, 8, 0, 0, 8, 0, 0, 0, 0, 40, 100, 3, 20, 0, 0, 40, 0, 40, 100, 20, 0, 0, 0, 0,
)
START_MIB, FORE_MIB, BACK_MIB = 44, 44, 44
NN = (((1,), (0,)), ((), ()))
NT = (((1,), (1,)), ((), ()))
TN = (((0,), (0,)), ((), ()))
VMEM = pl.BlockSpec(memory_space=pltpu.VMEM)
SMEM = pl.BlockSpec(memory_space=pltpu.SMEM)
ANY = pl.BlockSpec(memory_space=pl.ANY)


def cost(flops, nbytes):
    return pl.CostEstimate(flops=int(flops), bytes_accessed=int(nbytes), transcendentals=0)


def params(mib):
    return pltpu.CompilerParams(vmem_limit_bytes=mib * 1024 * 1024)


def matmul(a, b, dims=NN):
    return lax.dot_general(a, b, dims, preferred_element_type=F32)


def order(label, tokens, block):
    p = lax.broadcasted_iota(jnp.int32, (tokens, tokens), 0)
    t = lax.broadcasted_iota(jnp.int32, (tokens, tokens), 1)
    return ((p // block) ^ label) * block + p % block == t


def split_rows(part, swapped):
    half = part.shape[0] // 2
    if not swapped:
        return part[:half], part[half:]
    q = half // 2
    return (
        jnp.concatenate([part[:q], part[half : half + q]], axis=0),
        jnp.concatenate([part[q:half], part[half + q :]], axis=0),
    )


def join_rows(own, other, swapped):
    if not swapped:
        return jnp.concatenate([own, other], axis=0)
    q = own.shape[0] // 2
    return jnp.concatenate([own[:q], other[:q], own[q:], other[q:]], axis=0)


def start_kernel(block, span, tile, swapped, label, ids, excluded, gain, store, grad_out, w_down, w_gate, w_up, *rest):
    rows, dout, scaled, flipped, keep, send, pool_buf, grad_buf, wd, wg, wu, sems, w_sems = rest
    copies = [
        pltpu.make_async_copy(store, pool_buf, sems.at[0]),
        pltpu.make_async_copy(grad_out, grad_buf, sems.at[1]),
    ]
    w_copies = []
    for at in range(0, span[1], tile):
        there, here = pl.ds(span[0] + at, tile), pl.ds(at, tile)
        n = len(w_copies)
        w_copies.append(pltpu.make_async_copy(w_down.at[there], wd.at[here], w_sems.at[n]))
        w_copies.append(pltpu.make_async_copy(w_gate.at[:, there], wg.at[:, here], w_sems.at[n + 1]))
        w_copies.append(pltpu.make_async_copy(w_up.at[:, there], wu.at[:, here], w_sems.at[n + 2]))
    for copy in copies + w_copies:
        copy.start()
    tokens = grad_buf.shape[0]
    pool = pool_buf.shape[0]
    perm = jnp.where(order(label[0], tokens, block), 1.0, 0.0).astype(BF16)
    position = lax.broadcasted_iota(jnp.int32, (tokens, excluded.shape[1]), 0)
    match = jnp.where(position == excluded[...], 1.0, 0.0)
    dropped = jnp.max(match, axis=1, keepdims=True) > 0.0
    hit = lax.broadcasted_iota(jnp.int32, (pool, tokens), 0) == ids[...]
    hit = jnp.where(hit, 1.0, 0.0).astype(BF16)
    copies[0].wait()
    natural = matmul(hit, pool_buf[...], TN)
    row = matmul(perm, natural.astype(BF16))
    squares = jnp.broadcast_to(jnp.sum(row * row, axis=1, keepdims=True), (tokens, 128))
    put_pieces(*split_rows(squares, swapped), keep, send, span[1])
    rows[...] = row.astype(BF16)
    value = (row * gain[...]).astype(BF16)
    scaled[...] = value
    flipped[...] = jnp.transpose(value.astype(F32)).astype(BF16)
    copies[1].wait()
    kept = jnp.where(dropped, 0.0, grad_buf[...].astype(F32)).astype(BF16)
    dout[...] = matmul(perm, kept).astype(BF16)
    for n, copy in enumerate(w_copies):
        copy.wait()
        k = n % 3
        here = slice(n // 3 * tile, (n // 3 + 1) * tile)
        part = matmul(dout[...], wd[here], NT) if k == 0 else matmul(scaled[...], (wg if k == 1 else wu)[:, here])
        kept, sent = split_rows(part, swapped)
        keep[k, :, here] = kept
        send[k, :, here] = sent.astype(BF16)


def put_pieces(kept, sent, keep, send, at):
    for k in range(3):
        keep[k, :, at:] = kept if k == 0 else jnp.zeros_like(kept)
        piece = sent.astype(BF16)
        send[k, :, at:] = piece
        sent = sent - piece.astype(F32)


def fore_kernel(swapped, refs, keep, send):
    for k, (x, w, dims) in enumerate(refs):
        kept, sent = split_rows(matmul(x[...], w[...], dims), swapped)
        keep[k] = kept
        send[k] = sent.astype(BF16)


def all_kernel(swapped, normed, dout, w_down, w_gate, w_up, *rest):
    fore_kernel(swapped, [(dout, w_down, NT), (normed, w_gate, NN), (normed, w_up, NN)], *rest[-2:])


def halve_kernel(part, kept, received, *rest):
    keep, send = rest[-2:]
    rows = keep.shape[1]
    for k in range(3):
        total = kept[k, :, :part] + received[k, :, :part].astype(F32)
        keep[k, :, :part] = total[:rows]
        send[k, :, :part] = total[rows:].astype(BF16)
    if keep.shape[2] > part:
        total = sum(kept[k, :, part:] + received[k, :, part:].astype(F32) for k in range(3))
        put_pieces(total[:rows], total[rows:], keep, send, part)


def swiglu_kernel(part, last, width, kept, received, inner, inv_rms, *rest):
    acts, inner_out, inv_out = rest[-3:]
    d_hidden, gate_pre, up_proj = (kept[k, :, :part] + received[k, :, :part].astype(F32) for k in range(3))
    if kept.shape[2] > part:
        squares = sum(kept[k, :, part:] + received[k, :, part:].astype(F32) for k in range(3))
        inv = lax.rsqrt(squares / width + EPS)
    else:
        inv = inv_rms[...]
    inv_out[...] = inv
    inv = inv[:, :1]
    gate_pre = gate_pre * inv
    up_proj = up_proj * inv
    sigmoid_gate = jax.nn.sigmoid(gate_pre)
    silu = gate_pre * sigmoid_gate
    d_scaled = d_hidden * inv
    d_gate = (d_scaled * up_proj * sigmoid_gate * (1.0 + gate_pre * (1.0 - sigmoid_gate))).astype(BF16)
    d_up = (d_scaled * silu).astype(BF16)
    acts[0, :, :part] = (silu * up_proj).astype(BF16)
    acts[1, :, :part] = d_gate
    acts[2, :, :part] = d_up
    terms = d_gate.astype(F32) * gate_pre + d_up.astype(F32) * up_proj
    total = inner[...] + jnp.broadcast_to(inv * jnp.sum(terms, axis=1, keepdims=True), inner.shape)
    inner_out[...] = total
    if last:
        for k in range(3):
            piece = total.astype(BF16)
            acts[k, :, part:] = piece
            total = total - piece.astype(F32)


def join_kernel(own, other, *rest):
    rows = own.shape[1]
    out = rest[-1]
    out[:, :rows] = own[...]
    out[:, rows:] = other[...]


def back_kernel(first, last, swapped, own, other, flipped, dout, w_gate, w_up, w_down, *rest):
    acc, gate_grad, up_grad, down_grad = rest[-4:]
    tokens = dout.shape[0]
    step = pl.program_id(0)

    @pl.when(step == 0)
    def _():
        acc[...] = jnp.zeros_like(acc) if first else rest[0][...]

    hidden, d_gate, d_up = (join_rows(own[k], other[k], swapped) for k in range(3))
    gate_grad[...] = matmul(flipped[...], d_gate).astype(BF16)
    up_grad[...] = matmul(flipped[...], d_up).astype(BF16)
    down_grad[...] = matmul(hidden, dout[...], TN).astype(BF16)
    acc[:tokens] += matmul(hidden, w_down[...])
    acc[tokens : 2 * tokens] += matmul(d_gate, w_gate[...], NT) + matmul(d_up, w_up[...], NT)
    if last:

        @pl.when(step == 0)
        def _():
            places = 0 if first else 4
            pieces = [sum(x[k].astype(F32) for k in range(3)) for x in rest[places : places + 2]]
            inner = jnp.transpose(join_rows(*pieces, swapped))[:8]
            acc[2 * tokens :, :tokens] = inner


def end_kernel(block, width, label, own, other, rows, dout, gain, ids, output, store_grad, gain_grad):
    tokens = rows.shape[0]
    pool = store_grad.shape[0]
    places = order(label[0], tokens, block)
    perm = jnp.where(places, 1.0, 0.0).astype(BF16)
    here = lax.broadcasted_iota(jnp.int32, (tokens, tokens), 0) == lax.broadcasted_iota(jnp.int32, (tokens, tokens), 1)
    inner = own[2 * tokens : 2 * tokens + 1, :tokens] + other[2 * tokens : 2 * tokens + 1, :tokens]
    inner = jnp.sum(jnp.where(here, inner, 0.0), axis=1, keepdims=True)
    row = rows[...].astype(F32)
    result = (row + (own[:tokens] + other[:tokens])).astype(BF16)
    output[...] = matmul(perm, result, TN).astype(BF16)
    d_normed = own[tokens : 2 * tokens] + other[tokens : 2 * tokens]
    gain_grad[...] = jnp.sum(d_normed * row, axis=0, keepdims=True)
    d_rows = dout[...].astype(F32) + d_normed * gain[...] - row * (inner / width)
    hit = lax.broadcasted_iota(jnp.int32, (pool, tokens), 0) == ids[...]
    target = matmul(jnp.where(hit, 1.0, 0.0).astype(BF16), perm, NT).astype(BF16)
    total = jnp.zeros(store_grad.shape, F32)
    for _ in range(3):
        piece = d_rows.astype(BF16)
        total += matmul(target, piece)
        d_rows = d_rows - piece.astype(F32)
    store_grad[...] = total.astype(BF16)


def shards(sizes, replay_store, replay_ids, excluded, norm_gain, w_gate, w_up, w_down, grad_out):
    ways = sizes["width"]
    steps = ways.bit_length() - 1
    tokens, d_here = grad_out.shape
    ff = w_down.shape[0]
    width = ways * d_here
    block = tokens // ways
    half = tokens // 2
    pool = replay_store.shape[0]
    tile = ff // sum(COUNTS)
    shape = jax.ShapeDtypeStruct

    index = lax.axis_index("width")
    label = sum(((index >> s) & 1) << (steps - 1 - s) for s in range(steps))
    label = jnp.reshape(label, (1,)).astype(jnp.int32)

    def swap(x, step):
        return lax.ppermute(x, "width", [(i, i ^ (1 << step)) for i in range(ways)])

    def swap_cores(x):
        n = sizes["hidden"]
        return lax.ppermute(x, "hidden", [(i, (i + 1) % n) for i in range(n)])

    ids = replay_ids.reshape(1, tokens)
    gain = norm_gain.reshape(1, d_here)
    routes = [[1, 0, *range(2, steps)] if swapped else list(range(steps)) for swapped in SWAPPED]
    chunks = len(COUNTS)
    parts = [count * tile for count in COUNTS]
    firsts = [sum(parts[:j]) for j in range(chunks)]
    token, held, arrived = [], [], {}

    state = {"cost": 0}

    def kernel(body, out_shape, in_specs, out_specs, ins, name, mib=24, **more):
        after = token[-1:] + held
        held.clear()
        outs = pl.pallas_call(
            body,
            out_shape=out_shape,
            in_specs=list(in_specs) + [ANY] * len(after),
            out_specs=out_specs,
            compiler_params=params(mib),
            cost_estimate=cost(0, 1e6 * state["cost"]),
            name=name,
            **more,
        )(*ins, *after)
        token.append(outs[0])
        return outs

    part = parts[0]
    side = pltpu.VMEM((d_here, part), BF16)
    rows, dout, scaled, flipped, keep, send = kernel(
        functools.partial(start_kernel, block, (firsts[0], part), tile, SWAPPED[0]),
        (
            shape((tokens, d_here), BF16),
            shape((tokens, d_here), BF16),
            shape((tokens, d_here), BF16),
            shape((d_here, tokens), BF16),
            shape((3, half, part + 128), F32),
            shape((3, half, part + 128), BF16),
        ),
        [SMEM, VMEM, VMEM, VMEM] + [ANY] * 5,
        (VMEM,) * 6,
        [label, ids, excluded.reshape(1, -1), gain, replay_store, grad_out, w_down, w_gate, w_up],
        "start",
        mib=START_MIB,
        scratch_shapes=[
            pltpu.VMEM((pool, d_here), BF16),
            pltpu.VMEM((tokens, d_here), BF16),
            pltpu.VMEM((part, d_here), BF16),
            side,
            side,
            pltpu.SemaphoreType.DMA((2,)),
            pltpu.SemaphoreType.DMA((3 * COUNTS[0],)),
        ],
    )
    zeros = jnp.zeros((block, 128), F32)
    state |= {"inner": zeros, "inv": zeros, "acc": None, "grads": None, "swiglu": 0, "back": 0}
    arrived["F", 0] = swap(send, routes[0][0])
    sums, acts, others = {0: (keep, arrived["F", 0])}, {}, {}

    def fore(j):
        part = parts[j]
        whole = pl.BlockSpec((tokens, d_here), lambda i: (0, 0))
        col = pl.BlockSpec((d_here, tile), lambda i: (0, firsts[j] // tile + i))
        row = pl.BlockSpec((tile, d_here), lambda i: (firsts[j] // tile + i, 0))
        n = 3
        out = pl.BlockSpec((n, half, tile), lambda i: (0, 0, i))
        keep, send = kernel(
            functools.partial(all_kernel, SWAPPED[j]),
            (shape((n, half, part), F32), shape((n, half, part), BF16)),
            [whole, whole, row, col, col],
            (out, out),
            [scaled, dout, w_down, w_gate, w_up],
            "fore",
            mib=FORE_MIB,
            grid=(COUNTS[j],),
        )
        arrived["F", j] = swap(send, routes[j][0])
        sums[j] = keep, arrived["F", j]

    def halve(j, at):
        for step in range(at, steps - 1 if at else 1):
            kept, received = sums[j]
            here = (3, kept.shape[1] // 2, kept.shape[2])
            keep, send = kernel(
                functools.partial(halve_kernel, parts[j]),
                (shape(here, F32), shape(here, BF16)),
                [VMEM, VMEM],
                (VMEM, VMEM),
                [kept, received],
                "halve",
            )
            arrived["H", j, at] = swap(send, routes[j][step + 1])
            sums[j] = keep, arrived["H", j, at]

    def swiglu(j):
        state["swiglu"] += 1
        last = state["swiglu"] == chunks
        state["last"] = j if last else None
        acts[j], state["inner"], state["inv"] = kernel(
            functools.partial(swiglu_kernel, parts[j], last, width),
            (shape((3, block, parts[j] + (128 if last else 0)), BF16), shape((block, 128), F32), shape((block, 128), F32)),
            [VMEM] * 4,
            (VMEM,) * 3,
            [*sums[j], state["inner"], state["inv"]],
            "swiglu",
        )
        others[j] = arrived["W", j] = swap(acts[j], routes[j][steps - 1])

    def join(j, at):
        for step in reversed(range(at, steps if at > 1 else 2)):
            own, other = acts[j], others[j]
            if own.shape[1] % 16:
                acts[j] = jnp.concatenate([own, other], axis=1)
            else:
                (acts[j],) = kernel(
                    join_kernel,
                    (shape((3, 2 * own.shape[1], own.shape[2]), BF16),),
                    [VMEM, VMEM],
                    (VMEM,),
                    [own, other],
                    "join",
                )
            others[j] = arrived["J", j, at] = swap(acts[j], routes[j][step - 1])

    def back(j):
        state["back"] += 1
        first, last = state["back"] == 1, j == state["last"]
        own, other = acts[j], others[j]
        start = firsts[j] // tile
        col = pl.BlockSpec((d_here, tile), lambda i: (0, start + i))
        row = pl.BlockSpec((tile, d_here), lambda i: (start + i, 0))
        whole = lambda i: (0, 0)
        acc_spec = pl.BlockSpec((2 * tokens + 8, d_here), whole)
        piece = pl.BlockSpec((3, half, tile), lambda i: (0, 0, i))
        ins = [own, other, flipped, dout, w_gate, w_up, w_down]
        specs = [
            piece,
            piece,
            pl.BlockSpec((d_here, tokens), whole),
            pl.BlockSpec((tokens, d_here), whole),
            col,
            col,
            row,
        ]
        alias = {}
        if not first:
            ins += [state["acc"], *state["grads"]]
            specs += [acc_spec, ANY, ANY, ANY]
            alias = {8: 1, 9: 2, 10: 3}
        if last:
            extra = pl.BlockSpec((3, half, 128), lambda i: (0, 0, parts[j] // 128))
            ins += [own, other]
            specs += [extra, extra]
        state["acc"], *state["grads"] = kernel(
            functools.partial(back_kernel, first, last, SWAPPED[j]),
            (
                shape((2 * tokens + 8, d_here), F32),
                shape((d_here, ff), BF16),
                shape((d_here, ff), BF16),
                shape((ff, d_here), BF16),
            ),
            specs,
            (acc_spec, col, col, row),
            ins,
            "back",
            mib=BACK_MIB,
            grid=(COUNTS[j],),
            input_output_aliases=alias,
        )

    tasks = {"F": fore, "H": halve, "W": swiglu, "J": join, "B": back}
    for (task, *where), state["cost"] in zip(ORDER, COSTS):
        if task == "A":
            held.append(arrived[tuple(where)])
        else:
            tasks[task](*where)
    acc, grads = state["acc"], state["grads"]

    other = swap_cores(acc)
    output, store_grad, gain_grad = pl.pallas_call(
        functools.partial(end_kernel, block, width),
        out_shape=(shape((tokens, d_here), BF16), shape((pool, d_here), BF16), shape((1, d_here), F32)),
        in_specs=[SMEM] + [VMEM] * 6,
        out_specs=(VMEM, VMEM, VMEM),
        compiler_params=params(32),
        cost_estimate=cost(2 * tokens * pool * d_here, 16 * tokens * d_here),
        name="end",
    )(label, acc, other, rows, dout, gain, ids)
    return (output, store_grad, gain_grad.reshape(d_here), *grads)


def solution(mesh):
    return jax.shard_map(
        functools.partial(shards, dict(mesh.shape)),
        mesh=mesh,
        in_specs=(
            P("groups", "width"),
            P("groups"),
            P("groups"),
            P("width"),
            P("width", "hidden"),
            P("width", "hidden"),
            P("hidden", "width"),
            P("groups", "width"),
        ),
        out_specs=(
            P("groups", "width"),
            P("groups", "width"),
            P(("groups", "width")),
            P(("groups", "width"), "hidden"),
            P(("groups", "width"), "hidden"),
            P(("groups", "hidden"), "width"),
        ),
        check_vma=False,
    )
```
